32 devices in a mesh: groups: 2 (over x), lat: 16 (over z, y, core).
Axes of the slice: x: 2, y: 2, z: 4, core: 2. Of those that a mesh axis runs over, the one named last changes fastest.
Arguments:
- objects: float32 [2, 2, 8192, 1024], P(None, None, ('groups', 'lat')), parts along dimension 2, may hold values from -5 to 5
- probes: float32 [4, 2, 256, 256], P('groups'), parts along dimension 0, may hold values from -5 to 5
- x_offsets: int32 [64], P(('groups', 'lat')), parts along dimension 0, may hold values from 0 to 255
- y_offsets: int32 [64], P(('groups', 'lat')), parts along dimension 0, may hold values from 0 to 768
- modes: int32 [64], P(('groups', 'lat')), parts along dimension 0, may hold values from 0 to 1
- measured: float32 [64, 256, 256], P(('groups', 'lat')), parts along dimension 0, may hold values from 0 to 2
Outputs:
- updated: float32 [2, 2, 8192, 1024], P(None, None, ('groups', 'lat')), parts along dimension 2
The draws below stay inside these ranges and needn't reach their ends.
There are 2 independent parts, one for each index of `groups`. The reference program is written for one: setup_inputs(seed, part) draws one part's arguments, and reference() takes and returns one part's arrays. A program takes and returns all parts, laid end to end along the dimension named above; each array names one. Nothing has to cross between parts.
All inputs are finite; a program needn't handle non-finite values.
Results may differ from the reference program's by a relative error of at most 0.0003.
Values sent between devices are 32-bit elements; how exact they have to be, the bound alone decides.
A program may use at most 128 MiB of HBM per device.

```python
import jax
import jax.numpy as jnp
from jax import lax

W = 256
TILE = 256
OY = 1024
POS_DEV = 2
SLICES = 2
NPROBE = 2
NX = 4096
NPOS = 32
N_LAT = 16


def touch_ends(values, own_key, low, top_value):
    longest = values.shape.index(max(values.shape))
    spots = []
    for shift in (0, 1):
        where = [jax.random.randint(jax.random.fold_in(own_key, axis), (), 0, length) for axis, length in enumerate(values.shape)]
        where[longest] = (where[longest] + shift) % values.shape[longest]
        spots.append(tuple(where))
    return values.at[spots[0]].set(low).at[spots[1]].set(top_value)


def shard_levels(rng, dims, split, smallest, high):
    loudness = 1.0
    for dim, shards_of in split:
        heights = jax.random.uniform(jax.random.fold_in(jax.random.fold_in(rng, 6), dim), (shards_of,), jnp.float32, smallest / len(split), high / len(split))
        loudness = loudness * jnp.repeat(jnp.exp(heights), dims[dim] // shards_of).reshape((-1,) + (1,) * (len(dims) - 1 - dim))
    return loudness


def noise(own_key, dims, deviation, reach, shards=(), held_as=jnp.bfloat16):
    level = shard_levels(own_key, dims, shards, -0.22, 0.18) if shards else 1.0
    array = jax.random.normal(own_key, dims, jnp.float32) * deviation * level
    return jnp.minimum(jnp.maximum(array, -reach), reach).astype(held_as)


def setup_inputs(seed: int = 0, part: int = 0) -> dict:
    seeds = jax.random.split(jax.random.key(seed), 7)
    part_keys = jax.random.split(jax.random.fold_in(seeds[6], part), 7)
    objects = noise(part_keys[0], (SLICES, 2, NX, OY), 0.7, 5.0, ((2, 16),), jnp.float32)
    probes = noise(part_keys[1], (NPROBE, 2, W, W), 0.7, 5.0, (), jnp.float32)
    x_offsets = touch_ends(jax.random.randint(part_keys[2], (NPOS,), 0, TILE), jax.random.fold_in(part_keys[2], 1), 0, TILE - 1).astype(jnp.int32)
    y_offsets = touch_ends(jax.random.randint(part_keys[3], (NPOS,), 0, OY - W + 1), jax.random.fold_in(part_keys[3], 1), 0, OY - W).astype(jnp.int32)
    modes = touch_ends(jax.random.randint(part_keys[4], (NPOS,), 0, NPROBE), jax.random.fold_in(part_keys[4], 1), 0, NPROBE - 1).astype(jnp.int32)
    measured = jnp.clip(2.0 * jax.random.uniform(part_keys[5], (NPOS, W, W), jnp.float32) ** shard_levels(part_keys[5], (NPOS, W, W), ((0, 16),), -0.2, 0.2), 0.0, 2.0)
    return dict(objects=objects, probes=probes, x_offsets=x_offsets, y_offsets=y_offsets, modes=modes, measured=measured)


spread_phase = 40.0
descent_rate = 1.0


def kernel_phase(width):
    counter = jnp.arange(width, dtype=jnp.int32)
    folded = ((counter + width // 2) % width - width // 2).astype(jnp.float32) / width
    return spread_phase * (folded[:, None] ** 2 + folded[None, :] ** 2)


def propagate(wavefield, kernel):
    return jnp.fft.ifft2(jnp.fft.fft2(wavefield, norm="ortho") * kernel, norm="ortho")


def reference(objects, probes, x_offsets, y_offsets, modes, measured):
    transmission = objects[:, 0] + 1j * objects[:, 1]
    padded = jnp.concatenate([transmission, jnp.zeros_like(transmission[:, :TILE])], axis=1)
    probe_field = probes[:, 0] + 1j * probes[:, 1]
    forward_kernel = jnp.exp(-1j * kernel_phase(W))
    anchor = jnp.zeros((), jnp.int32)
    positions = jnp.arange(POS_DEV * N_LAT, dtype=jnp.int32)

    def visit(gradient, record):
        position, x_offset, y_offset, probe_mode, intensity = record
        corner = (anchor, (position // POS_DEV) * TILE + x_offset, y_offset)
        window = lax.dynamic_slice(padded, corner, (SLICES, W, W))
        wavefield = probe_field[probe_mode]
        entering = []
        for s in range(SLICES):
            if s > 0:
                wavefield = propagate(wavefield, forward_kernel)
            entering.append(wavefield)
            wavefield = wavefield * window[s]
        detector = jnp.fft.fft2(wavefield, norm="ortho")
        residual = detector.real ** 2 + detector.imag ** 2 - intensity
        adjoint = jnp.fft.ifft2(residual * detector, norm="ortho")
        pieces = [None] * SLICES
        for s in reversed(range(SLICES)):
            pieces[s] = jnp.conj(entering[s]) * adjoint
            adjoint = jnp.conj(window[s]) * adjoint
            if s > 0:
                adjoint = propagate(adjoint, jnp.conj(forward_kernel))
        current = lax.dynamic_slice(gradient, corner, (SLICES, W, W))
        return lax.dynamic_update_slice(gradient, current + jnp.stack(pieces), corner), None

    gradient, _ = lax.scan(visit, jnp.zeros_like(padded), (positions, x_offsets, y_offsets, modes, measured))
    gradient = gradient[:, :NX]
    updated = transmission - descent_rate * gradient
    return jnp.stack([updated.real, updated.imag], axis=1).astype(jnp.float32)
```

```python
import functools

import jax
import jax.numpy as jnp
import ml_dtypes
import numpy as np
from jax import lax
from jax.experimental import pallas as pl
from jax.experimental.pallas import tpu as pltpu
from jax.sharding import PartitionSpec as P

spread_phase = 40.0
descent_rate = 1.0
VMEM_BYTES = 48 * 1024 * 1024


def from_behind(block, axis, distance):
    devices = range(lax.axis_size(axis))
    route = [(i - distance, i) for i in devices if i - distance in devices]
    return lax.ppermute(block, axis, route)


def split_table(table):
    high = table.astype(ml_dtypes.bfloat16)
    low = (table - high.astype(np.float64)).astype(ml_dtypes.bfloat16)
    return high, low


def tables(width):
    counter = np.arange(width)
    fourier = np.exp(-2j * np.pi * (np.outer(counter, counter) % width) / width) / np.sqrt(width)
    folded = ((counter + width // 2) % width - width // 2) / width
    phase = np.exp(-1j * spread_phase * folded**2)
    moving = np.conj(fourier) @ (phase[:, None] * fourier)
    rights, lefts = [], []
    for matrix in (moving, fourier):
        real, imag = matrix.real, matrix.imag
        high, low = split_table(np.block([[real, imag], [-imag, real]]))
        rights.append(np.concatenate([high, high, low], axis=0))
        high, low = split_table(np.block([[real, -imag], [imag, real]]))
        lefts.append(np.concatenate([high, high, low], axis=1))
    return np.stack(rights), np.stack(lefts)


def halves(values):
    high = values.astype(jnp.bfloat16)
    low = (values - high.astype(jnp.float32)).astype(jnp.bfloat16)
    return high, low


def transform(real, imag, right, left):
    width = real.shape[0]
    high, low = halves(jnp.concatenate([real, imag], axis=1))
    rows = jnp.dot(
        jnp.concatenate([high, low, high], axis=1), right, preferred_element_type=jnp.float32
    )
    high, low = halves(jnp.concatenate([rows[:, :width], rows[:, width:]], axis=0))
    both = jnp.dot(
        left, jnp.concatenate([high, low, high], axis=0), preferred_element_type=jnp.float32
    )
    return both[:width], both[width:]


def times(a, b):
    return a[0] * b[0] - a[1] * b[1], a[0] * b[1] + a[1] * b[0]


def pack_kernel(place, first, second, out):
    width = first.shape[-1]
    column = lax.broadcasted_iota(jnp.int32, (width, width), 1)
    turned = column < place[1] % width
    for s in range(first.shape[0]):
        for c in range(2):
            out[s, c] = jnp.where(turned, second[s, c], first[s, c])


def position_kernel(place, first, second, beyond, probe, measured, right, left, out):
    width = first.shape[-1]
    x, shift = place[0], place[1] % width
    row = lax.broadcasted_iota(jnp.int32, (width, width), 0)
    column = lax.broadcasted_iota(jnp.int32, (width, width), 1)
    inside, turned = row >= x, column < shift

    def window(s, c):
        own = jnp.where(turned, second[s, c], first[s, c])
        return jnp.where(inside, own, beyond[s, c])

    def rolled(c):
        return pltpu.roll(pltpu.roll(probe[0, c], x, 0), shift, 1)

    move, far = (right[0], left[0]), (right[1], left[1])
    entry = (rolled(0), rolled(1))
    slab = (window(1, 0), window(1, 1))
    middle = transform(*times(entry, (window(0, 0), window(0, 1))), *move)
    psi = transform(*times(middle, slab), *far)
    residual = psi[0] * psi[0] + psi[1] * psi[1] - measured[0]
    back = transform(residual * psi[0], -(residual * psi[1]), *far)
    piece = times(middle, back)
    out[1, 0] = piece[0]
    out[1, 1] = -piece[1]
    back = transform(*times(slab, back), *move)
    piece = times(entry, back)
    out[0, 0] = piece[0]
    out[0, 1] = -piece[1]


def update_kernel(places, objects, piece0, piece1, back0, back1, out):
    width = objects.shape[-1]
    block = pl.program_id(0)
    row = lax.broadcasted_iota(jnp.int32, (width, width), 0)
    column = lax.broadcasted_iota(jnp.int32, (width, width), 1) + block * width
    masks = []
    for k in range(4):
        x, y = places[k, 0], places[k, 1]
        across = (column >= y) & (column < y + width)
        masks.append(across & ((row >= x) if k < 2 else (row < x)))
    for s in range(objects.shape[0]):
        for c in range(2):
            total = objects[s, c]
            for mask, piece in zip(masks, (piece0, piece1, back0, back1)):
                total = total - descent_rate * jnp.where(mask, piece[s, c], 0.0)
            out[s, c] = total


def on_device(objects, probes, x_offsets, y_offsets, modes, measured):
    slices, _, tile, span = objects.shape
    width = measured.shape[1]
    blocks = span // width
    amount = x_offsets.shape[0]
    right, left = tables(width)
    right, left = jnp.asarray(right), jnp.asarray(left)
    window = (slices, 2, width, width)
    params = pltpu.CompilerParams(vmem_limit_bytes=VMEM_BYTES)

    own = jnp.stack([x_offsets, y_offsets, modes], axis=1)
    previous = from_behind(own, "lat", 1)

    lower = pl.BlockSpec(window, lambda i, place: (0, 0, 0, place[1] // width))
    upper = pl.BlockSpec(
        window, lambda i, place: (0, 0, 0, jnp.minimum(place[1] // width + 1, blocks - 1))
    )
    whole = pl.BlockSpec(window, lambda i, place: (0, 0, 0, 0))

    def pack(place):
        return pl.pallas_call(
            pack_kernel,
            grid_spec=pltpu.PrefetchScalarGridSpec(
                num_scalar_prefetch=1, grid=(1,), in_specs=[lower, upper], out_specs=whole
            ),
            out_shape=jax.ShapeDtypeStruct(window, jnp.float32),
            compiler_params=params,
            cost_estimate=pl.CostEstimate(flops=0, bytes_accessed=3 << 20, transcendentals=0),
            name="pack",
        )(place, objects, objects)

    def position(place, beyond, k):
        return pl.pallas_call(
            position_kernel,
            grid_spec=pltpu.PrefetchScalarGridSpec(
                num_scalar_prefetch=1,
                grid=(1,),
                in_specs=[
                    lower,
                    upper,
                    whole,
                    pl.BlockSpec((1, 2, width, width), lambda i, place: (place[2], 0, 0, 0)),
                    pl.BlockSpec((1, width, width), lambda i, place: (k, 0, 0)),
                    pl.BlockSpec(right.shape, lambda i, place: (0, 0, 0)),
                    pl.BlockSpec(left.shape, lambda i, place: (0, 0, 0)),
                ],
                out_specs=whole,
            ),
            out_shape=jax.ShapeDtypeStruct(window, jnp.float32),
            compiler_params=params,
            cost_estimate=pl.CostEstimate(
                flops=8 * 2 * 6 * 2 * width**3, bytes_accessed=10 << 20, transcendentals=0
            ),
            name="position",
        )(place, objects, objects, beyond, probes, measured, right, left)

    packed = [pack(previous[k]) for k in range(amount)]
    beyond = [from_behind(block, "lat", -1) for block in packed]
    pieces = [position(own[k], beyond[k], k) for k in range(amount)]
    returned = [from_behind(piece, "lat", 1) for piece in pieces]
    strip = pl.BlockSpec(window, lambda i, places: (0, 0, 0, i))
    fixed = pl.BlockSpec(window, lambda i, places: (0, 0, 0, 0))
    return pl.pallas_call(
        update_kernel,
        grid_spec=pltpu.PrefetchScalarGridSpec(
            num_scalar_prefetch=1,
            grid=(blocks,),
            in_specs=[strip] + [fixed] * 4,
            out_specs=strip,
        ),
        out_shape=jax.ShapeDtypeStruct(objects.shape, jnp.float32),
        compiler_params=params,
        name="update",
    )(jnp.concatenate([own, previous], axis=0), objects, *pieces, *returned)


def solution(mesh):
    in_specs = (
        P(None, None, ("groups", "lat"), None),
        P("groups", None, None, None),
        P(("groups", "lat")),
        P(("groups", "lat")),
        P(("groups", "lat")),
        P(("groups", "lat"), None, None),
    )
    out_specs = P(None, None, ("groups", "lat"), None)
    return jax.shard_map(
        on_device, mesh=mesh, in_specs=in_specs, out_specs=out_specs, check_vma=False
    )
```

```python
import jax
import jax.numpy as jnp
import numpy as np
from jax import lax
from jax.experimental import pallas as pl
from jax.experimental.pallas import tpu as pltpu
from jax.sharding import PartitionSpec as P

spread_phase = 40.0
descent_rate = 1.0
VMEM_BYTES = 60 * 1024 * 1024


def tables(width):
    counter = np.arange(width)
    fourier = np.exp(-2j * np.pi * (np.outer(counter, counter) % width) / width) / np.sqrt(width)
    folded = ((counter + width // 2) % width - width // 2) / width
    phase = np.exp(-1j * spread_phase * folded**2)
    moving = np.conj(fourier) @ (phase[:, None] * fourier)
    parts = [[matrix.real, matrix.imag] for matrix in (moving, fourier)]
    return np.array(parts, dtype=np.float32)


def halves(values):
    high = values.astype(jnp.bfloat16)
    low = (values - high.astype(jnp.float32)).astype(jnp.bfloat16)
    return high, low


def transform(real, imag, right, left):
    width = real.shape[0]
    high, low = halves(jnp.concatenate([real, imag], axis=1))
    rows = jnp.dot(
        jnp.concatenate([high, low, high], axis=1), right, preferred_element_type=jnp.float32
    )
    high, low = halves(jnp.concatenate([rows[:, :width], rows[:, width:]], axis=0))
    both = jnp.dot(
        left, jnp.concatenate([high, low, high], axis=0), preferred_element_type=jnp.float32
    )
    return both[:width], both[width:]


def times(a, b):
    return a[0] * b[0] - a[1] * b[1], a[0] * b[1] + a[1] * b[0]


def kernel(
    x_ref,
    y_ref,
    mode_ref,
    objects_hbm,
    probes_hbm,
    measured_hbm,
    tables_hbm,
    updated_hbm,
    objects,
    probes,
    measured,
    tables_f32,
    right,
    left,
    total,
    place,
    place_before,
    packed,
    beyond,
    pieces,
    returned,
    load_sem,
    place_sem,
    object_sem,
    piece_sem,
    store_sem,
):
    slices, _, tile, span = objects.shape
    amount, width, _ = measured.shape
    me, devices = lax.axis_index("lat"), lax.axis_size("lat")
    has_before, has_after = me > 0, me < devices - 1
    before, after = jnp.maximum(me - 1, 0), jnp.minimum(me + 1, devices - 1)

    def send(source, target, sems, towards):
        return pltpu.make_async_remote_copy(
            src_ref=source,
            dst_ref=target,
            send_sem=sems[0],
            recv_sem=sems[1],
            device_id={"lat": towards},
            device_id_type=pl.DeviceIdType.MESH,
        )

    def send_place():
        return send(place, place_before, (place_sem.at[0], place_sem.at[1]), after)

    def send_objects(p, s):
        sems = (object_sem.at[0, p, s], object_sem.at[1, p, s])
        return send(packed.at[p, s], beyond.at[p, s], sems, before)

    def send_piece(p, s):
        sems = (piece_sem.at[0, p, s], piece_sem.at[1, p, s])
        return send(pieces.at[p, s], returned.at[p, s], sems, after)

    load_objects = pltpu.make_async_copy(objects_hbm, objects, load_sem.at[0])
    others = [
        pltpu.make_async_copy(source, target, load_sem.at[i + 1])
        for i, (source, target) in enumerate(
            [(tables_hbm, tables_f32), (probes_hbm, probes), (measured_hbm, measured)]
        )
    ]
    load_objects.start()
    for p in range(amount):
        place[p] = jnp.full((1, width), x_ref[p], jnp.int32)
        place[amount + p] = jnp.full((1, width), y_ref[p], jnp.int32)

    barrier = pltpu.get_barrier_semaphore()

    @pl.when(has_before)
    def _():
        pl.semaphore_signal(
            barrier, inc=1, device_id={"lat": before}, device_id_type=pl.DeviceIdType.MESH
        )

    @pl.when(has_after)
    def _():
        pl.semaphore_signal(
            barrier, inc=1, device_id={"lat": after}, device_id_type=pl.DeviceIdType.MESH
        )

    peers = has_before.astype(jnp.int32) + has_after.astype(jnp.int32)
    pl.semaphore_wait(barrier, peers)

    @pl.when(has_after)
    def _():
        send_place().start()

    row = lax.broadcasted_iota(jnp.int32, (width, width), 0)
    column = lax.broadcasted_iota(jnp.int32, (width, width), 1)

    def across(y, k):
        return (column + k * width >= y) & (column + k * width < y + width)

    def gathered(y, s, c):
        value = objects[s, c, :, 0:width]
        for k in range(1, span // width):
            value = jnp.where(across(y, k), objects[s, c, :, k * width : (k + 1) * width], value)
        return value

    load_objects.wait()

    @pl.when(has_before)
    def _():
        send_place().wait_recv()

        def pack(p, carry):
            y = place_before[amount + p]
            for s in range(slices):
                for c in range(2):
                    packed[p, s, c] = gathered(y, s, c)
                send_objects(p, s).start()
            return carry

        lax.fori_loop(0, amount, pack, 0)

    for copy in others:
        copy.start()

    @pl.when(jnp.logical_not(has_after))
    def _():
        beyond[...] = jnp.zeros_like(beyond)

    for copy in others:
        copy.wait()

    for i in range(2):
        for c, sign in ((0, 1.0), (1, 1.0), (1, -1.0)):
            high, low = halves(sign * tables_f32[i, c])
            for k, part in enumerate((high, high, low)):
                base = 2 * width * k
                near, further = pl.ds(base, width), pl.ds(base + width, width)
                first, second = pl.ds(0, width), pl.ds(width, width)
                if c == 0:
                    right[i, near, first] = part
                    right[i, further, second] = part
                    left[i, first, near] = part
                    left[i, second, further] = part
                elif sign > 0:
                    right[i, near, second] = part
                    left[i, second, near] = part
                else:
                    right[i, further, first] = part
                    left[i, first, further] = part

    def visit(p, carry):
        x, y, mode = x_ref[p], y_ref[p], mode_ref[p]
        inside = row >= x
        shift = lax.rem(y, width)
        entry = [pltpu.roll(pltpu.roll(probes[mode, c], x, 0), shift, 1) for c in range(2)]

        def window(s):
            own = [gathered(y, s, c) for c in range(2)]

            @pl.when(has_after)
            def _():
                send_objects(p, s).wait_recv()

            return [jnp.where(inside, own[c], beyond[p, s, c]) for c in range(2)]

        def emit(s, piece):
            pieces[p, s, 0] = piece[0]
            pieces[p, s, 1] = -piece[1]

            @pl.when(has_after)
            def _():
                send_piece(p, s).start()

        move, far = (right[0], left[0]), (right[1], left[1])
        middle = transform(*times(entry, window(0)), *move)
        slab = window(1)
        psi = transform(*times(middle, slab), *far)
        residual = psi[0] * psi[0] + psi[1] * psi[1] - measured[p]
        back = transform(residual * psi[0], -(residual * psi[1]), *far)
        emit(1, times(middle, back))
        back = transform(*times(slab, back), *move)
        emit(0, times(entry, back))
        return carry

    lax.fori_loop(0, amount, visit, 0)

    def own_update(s, carry):
        for c in range(2):
            for k in range(span // width):
                value = objects[s, c, :, k * width : (k + 1) * width]
                for p in range(amount):
                    mask = across(y_ref[p], k) & (row >= x_ref[p])
                    value = value - descent_rate * jnp.where(mask, pieces[p, s, c], 0.0)
                total[s, c, :, k * width : (k + 1) * width] = value
        return carry

    lax.fori_loop(0, slices, own_update, 0)

    def store(s):
        return pltpu.make_async_copy(total.at[s], updated_hbm.at[s], store_sem.at[s])

    def late_update(step, carry):
        p, s = step // slices, slices - 1 - step % slices

        @pl.when(has_before)
        def _():
            send_piece(p, s).wait_recv()
            x, y = place_before[p], place_before[amount + p]
            inside = row < x
            for c in range(2):
                piece = jnp.where(inside, returned[p, s, c], 0.0)
                for k in range(span // width):
                    kept = jnp.where(across(y, k), piece, 0.0)
                    where = (s, c, slice(None), slice(k * width, (k + 1) * width))
                    total[where] = total[where] - descent_rate * kept

        @pl.when(p == amount - 1)
        def _():
            store(s).start()

        return carry

    lax.fori_loop(0, amount * slices, late_update, 0)

    for p in range(amount):
        for s in range(slices):

            @pl.when(has_before)
            def _():
                send_objects(p, s).wait_send()

            @pl.when(has_after)
            def _():
                send_piece(p, s).wait_send()

    @pl.when(has_after)
    def _():
        send_place().wait_send()

    for s in range(slices):
        store(s).wait()


def on_device(objects, probes, x_offsets, y_offsets, modes, measured):
    slices = objects.shape[0]
    amount, width, _ = measured.shape
    factors = jnp.asarray(tables(width))
    windows = (amount, slices, 2, width, width)
    small = pl.BlockSpec(memory_space=pltpu.SMEM)
    large = pl.BlockSpec(memory_space=pl.ANY)
    return pl.pallas_call(
        kernel,
        out_shape=jax.ShapeDtypeStruct(objects.shape, jnp.float32),
        in_specs=[small] * 3 + [large] * 4,
        out_specs=large,
        scratch_shapes=[
            pltpu.VMEM(objects.shape, jnp.float32),
            pltpu.VMEM(probes.shape, jnp.float32),
            pltpu.VMEM(measured.shape, jnp.float32),
            pltpu.VMEM(factors.shape, jnp.float32),
            pltpu.VMEM((2, 6 * width, 2 * width), jnp.bfloat16),
            pltpu.VMEM((2, 2 * width, 6 * width), jnp.bfloat16),
            pltpu.VMEM(objects.shape, jnp.float32),
            pltpu.VMEM((2 * amount, 1, width), jnp.int32),
            pltpu.VMEM((2 * amount, 1, width), jnp.int32),
            pltpu.VMEM(windows, jnp.float32),
            pltpu.VMEM(windows, jnp.float32),
            pltpu.VMEM(windows, jnp.float32),
            pltpu.VMEM(windows, jnp.float32),
            pltpu.SemaphoreType.DMA((4,)),
            pltpu.SemaphoreType.DMA((2,)),
            pltpu.SemaphoreType.DMA((2, amount, slices)),
            pltpu.SemaphoreType.DMA((2, amount, slices)),
            pltpu.SemaphoreType.DMA((slices,)),
        ],
        compiler_params=pltpu.CompilerParams(
            collective_id=0, has_side_effects=True, vmem_limit_bytes=VMEM_BYTES
        ),
        cost_estimate=pl.CostEstimate(
            flops=amount * 8 * 2 * 6 * 2 * width**3, bytes_accessed=16 << 20, transcendentals=0
        ),
        name="gradient_step",
    )(x_offsets, y_offsets, modes, objects, probes, measured, factors)


def solution(mesh):
    in_specs = (
        P(None, None, ("groups", "lat"), None),
        P("groups", None, None, None),
        P(("groups", "lat")),
        P(("groups", "lat")),
        P(("groups", "lat")),
        P(("groups", "lat"), None, None),
    )
    out_specs = P(None, None, ("groups", "lat"), None)
    return jax.shard_map(
        on_device, mesh=mesh, in_specs=in_specs, out_specs=out_specs, check_vma=False
    )
```

```python
import jax
import jax.numpy as jnp
import numpy as np
from jax import lax
from jax.experimental import pallas as pl
from jax.experimental.pallas import tpu as pltpu
from jax.sharding import PartitionSpec as P

spread_phase = 40.0
descent_rate = 1.0
VMEM_BYTES = 59 * 1024 * 1024


def tables(width):
    counter = np.arange(width)
    fourier = np.exp(-2j * np.pi * (np.outer(counter, counter) % width) / width) / np.sqrt(width)
    folded = ((counter + width // 2) % width - width // 2) / width
    phase = np.exp(-1j * spread_phase * folded**2)
    moving = np.conj(fourier) @ (phase[:, None] * fourier)
    parts = [[matrix.real, matrix.imag] for matrix in (moving, fourier)]
    return np.array(parts, dtype=np.float32)


def halves(values):
    high = values.astype(jnp.bfloat16)
    low = (values - high.astype(jnp.float32)).astype(jnp.bfloat16)
    return high, low


def transform(real, imag, right, left):
    width = real.shape[0]
    high, low = halves(jnp.concatenate([real, imag], axis=1))
    rows = jnp.dot(
        jnp.concatenate([high, low, high], axis=1), right, preferred_element_type=jnp.float32
    )
    high, low = halves(jnp.concatenate([rows[:, :width], rows[:, width:]], axis=0))
    both = jnp.dot(
        left, jnp.concatenate([high, low, high], axis=0), preferred_element_type=jnp.float32
    )
    return both[:width], both[width:]


def times(a, b):
    return a[0] * b[0] - a[1] * b[1], a[0] * b[1] + a[1] * b[0]


def kernel(
    x_ref,
    y_ref,
    mode_ref,
    objects_hbm,
    probes_hbm,
    measured_hbm,
    tables_hbm,
    updated_hbm,
    objects,
    probes,
    measured,
    tables_f32,
    right,
    left,
    total,
    place,
    place_before,
    packed,
    beyond,
    pieces,
    returned,
    load_sem,
    place_sem,
    object_sem,
    piece_sem,
    store_sem,
):
    slices, _, tile, span = objects.shape
    amount, width, _ = measured.shape
    me, devices = lax.axis_index("lat"), lax.axis_size("lat")
    has_before, has_after = me > 0, me < devices - 1
    before, after = jnp.maximum(me - 1, 0), jnp.minimum(me + 1, devices - 1)

    def send(source, target, sems, towards):
        return pltpu.make_async_remote_copy(
            src_ref=source,
            dst_ref=target,
            send_sem=sems[0],
            recv_sem=sems[1],
            device_id={"lat": towards},
            device_id_type=pl.DeviceIdType.MESH,
        )

    def send_place():
        return send(place, place_before, (place_sem.at[0], place_sem.at[1]), after)

    def send_objects(p, s):
        sems = (object_sem.at[0, p, s], object_sem.at[1, p, s])
        return send(packed.at[p, s], beyond.at[p, s], sems, before)

    def send_piece(p, s):
        sems = (piece_sem.at[0, p, s], piece_sem.at[1, p, s])
        return send(pieces.at[p, s], returned.at[p, s], sems, after)

    load_objects = pltpu.make_async_copy(objects_hbm, objects, load_sem.at[0])
    others = [
        pltpu.make_async_copy(source, target, load_sem.at[i + 1])
        for i, (source, target) in enumerate(
            [(tables_hbm, tables_f32), (probes_hbm, probes), (measured_hbm, measured)]
        )
    ]
    load_objects.start()
    for p in range(amount):
        place[p] = jnp.full((1, width), x_ref[p], jnp.int32)
        place[amount + p] = jnp.full((1, width), y_ref[p], jnp.int32)

    barrier = pltpu.get_barrier_semaphore()

    @pl.when(has_before)
    def _():
        pl.semaphore_signal(
            barrier, inc=1, device_id={"lat": before}, device_id_type=pl.DeviceIdType.MESH
        )

    @pl.when(has_after)
    def _():
        pl.semaphore_signal(
            barrier, inc=1, device_id={"lat": after}, device_id_type=pl.DeviceIdType.MESH
        )

    peers = has_before.astype(jnp.int32) + has_after.astype(jnp.int32)
    pl.semaphore_wait(barrier, peers)

    @pl.when(has_after)
    def _():
        send_place().start()

    row = lax.broadcasted_iota(jnp.int32, (width, width), 0)
    column = lax.broadcasted_iota(jnp.int32, (width, width), 1)

    def across(y, k):
        return (column + k * width >= y) & (column + k * width < y + width)

    def gathered(y, s, c):
        value = objects[s, c, :, 0:width]
        for k in range(1, span // width):
            value = jnp.where(across(y, k), objects[s, c, :, k * width : (k + 1) * width], value)
        return value

    load_objects.wait()

    @pl.when(has_before)
    def _():
        send_place().wait_recv()

        def pack(p, carry):
            y = place_before[amount + p]
            for s in range(slices):
                for c in range(2):
                    packed[p, s, c] = gathered(y, s, c)

                @pl.when(p == 0)
                def _():
                    send_objects(p, s).start()

            return carry

        lax.fori_loop(0, amount, pack, 0)

    for copy in others:
        copy.start()

    @pl.when(jnp.logical_not(has_after))
    def _():
        beyond[...] = jnp.zeros_like(beyond)

    for copy in others:
        copy.wait()

    for i in range(2):
        for c, sign in ((0, 1.0), (1, 1.0), (1, -1.0)):
            high, low = halves(sign * tables_f32[i, c])
            for k, part in enumerate((high, high, low)):
                base = 2 * width * k
                near, further = pl.ds(base, width), pl.ds(base + width, width)
                first, second = pl.ds(0, width), pl.ds(width, width)
                if c == 0:
                    right[i, near, first] = part
                    right[i, further, second] = part
                    left[i, first, near] = part
                    left[i, second, further] = part
                elif sign > 0:
                    right[i, near, second] = part
                    left[i, second, near] = part
                else:
                    right[i, further, first] = part
                    left[i, first, further] = part

    def visit(p, carry):
        @pl.when(has_before & (p + 1 < amount))
        def _():
            for s in range(slices):
                send_objects(p, s).wait_send()
                send_objects(p + 1, s).start()

        x, y, mode = x_ref[p], y_ref[p], mode_ref[p]
        inside = row >= x
        shift = lax.rem(y, width)
        entry = [pltpu.roll(pltpu.roll(probes[mode, c], x, 0), shift, 1) for c in range(2)]

        def window(s):
            own = [gathered(y, s, c) for c in range(2)]

            @pl.when(has_after)
            def _():
                send_objects(p, s).wait_recv()

            return [jnp.where(inside, own[c], beyond[p, s, c]) for c in range(2)]

        def emit(s, piece):
            pieces[p, s, 0] = piece[0]
            pieces[p, s, 1] = -piece[1]

            @pl.when(has_after)
            def _():
                send_piece(p, s).start()

        move, far = (right[0], left[0]), (right[1], left[1])
        middle = transform(*times(entry, window(0)), *move)
        slab = window(1)
        psi = transform(*times(middle, slab), *far)
        residual = psi[0] * psi[0] + psi[1] * psi[1] - measured[p]
        back = transform(residual * psi[0], -(residual * psi[1]), *far)
        emit(1, times(middle, back))
        back = transform(*times(slab, back), *move)
        emit(0, times(entry, back))
        return carry

    lax.fori_loop(0, amount, visit, 0)

    def own_update(s, carry):
        for c in range(2):
            for k in range(span // width):
                value = objects[s, c, :, k * width : (k + 1) * width]
                for p in range(amount):
                    mask = across(y_ref[p], k) & (row >= x_ref[p])
                    value = value - descent_rate * jnp.where(mask, pieces[p, s, c], 0.0)
                total[s, c, :, k * width : (k + 1) * width] = value
        return carry

    lax.fori_loop(0, slices, own_update, 0)

    def store(s):
        return pltpu.make_async_copy(total.at[s], updated_hbm.at[s], store_sem.at[s])

    def late_update(step, carry):
        p, s = step // slices, slices - 1 - step % slices

        @pl.when(has_before)
        def _():
            send_piece(p, s).wait_recv()
            x, y = place_before[p], place_before[amount + p]
            inside = row < x
            for c in range(2):
                piece = jnp.where(inside, returned[p, s, c], 0.0)
                for k in range(span // width):
                    kept = jnp.where(across(y, k), piece, 0.0)
                    where = (s, c, slice(None), slice(k * width, (k + 1) * width))
                    total[where] = total[where] - descent_rate * kept

        @pl.when(p == amount - 1)
        def _():
            store(s).start()

        return carry

    lax.fori_loop(0, amount * slices, late_update, 0)

    for s in range(slices):

        @pl.when(has_before)
        def _():
            send_objects(amount - 1, s).wait_send()

        for p in range(amount):

            @pl.when(has_after)
            def _():
                send_piece(p, s).wait_send()

    @pl.when(has_after)
    def _():
        send_place().wait_send()

    for s in range(slices):
        store(s).wait()


def on_device(objects, probes, x_offsets, y_offsets, modes, measured):
    slices = objects.shape[0]
    amount, width, _ = measured.shape
    factors = jnp.asarray(tables(width))
    windows = (amount, slices, 2, width, width)
    small = pl.BlockSpec(memory_space=pltpu.SMEM)
    large = pl.BlockSpec(memory_space=pltpu.HBM)
    return pl.pallas_call(
        kernel,
        out_shape=pltpu.VMEM(objects.shape, jnp.float32),
        in_specs=[small] * 3 + [large] * 4,
        out_specs=pl.BlockSpec(memory_space=pl.ANY),
        scratch_shapes=[
            pltpu.VMEM(objects.shape, jnp.float32),
            pltpu.VMEM(probes.shape, jnp.float32),
            pltpu.VMEM(measured.shape, jnp.float32),
            pltpu.VMEM(factors.shape, jnp.float32),
            pltpu.VMEM((2, 6 * width, 2 * width), jnp.bfloat16),
            pltpu.VMEM((2, 2 * width, 6 * width), jnp.bfloat16),
            pltpu.VMEM(objects.shape, jnp.float32),
            pltpu.VMEM((2 * amount, 1, width), jnp.int32),
            pltpu.VMEM((2 * amount, 1, width), jnp.int32),
            pltpu.VMEM(windows, jnp.float32),
            pltpu.VMEM(windows, jnp.float32),
            pltpu.VMEM(windows, jnp.float32),
            pltpu.VMEM(windows, jnp.float32),
            pltpu.SemaphoreType.DMA((4,)),
            pltpu.SemaphoreType.DMA((2,)),
            pltpu.SemaphoreType.DMA((2, amount, slices)),
            pltpu.SemaphoreType.DMA((2, amount, slices)),
            pltpu.SemaphoreType.DMA((slices,)),
        ],
        compiler_params=pltpu.CompilerParams(
            collective_id=0, has_side_effects=True, vmem_limit_bytes=VMEM_BYTES
        ),
        cost_estimate=pl.CostEstimate(
            flops=amount * 8 * 2 * 6 * 2 * width**3, bytes_accessed=16 << 20, transcendentals=0
        ),
        name="gradient_step",
    )(x_offsets, y_offsets, modes, objects, probes, measured, factors)


def solution(mesh):
    in_specs = (
        P(None, None, ("groups", "lat"), None),
        P("groups", None, None, None),
        P(("groups", "lat")),
        P(("groups", "lat")),
        P(("groups", "lat")),
        P(("groups", "lat"), None, None),
    )
    out_specs = P(None, None, ("groups", "lat"), None)
    return jax.shard_map(
        on_device, mesh=mesh, in_specs=in_specs, out_specs=out_specs, check_vma=False
    )
```

```python
import jax
import jax.numpy as jnp
import numpy as np
from jax import lax
from jax.experimental import pallas as pl
from jax.experimental.pallas import tpu as pltpu
from jax.sharding import PartitionSpec as P

spread_phase = 40.0
descent_rate = 1.0
VMEM_BYTES = 59 * 1024 * 1024


def tables(width):
    counter = np.arange(width)
    fourier = np.exp(-2j * np.pi * (np.outer(counter, counter) % width) / width) / np.sqrt(width)
    folded = ((counter + width // 2) % width - width // 2) / width
    phase = np.exp(-1j * spread_phase * folded**2)
    moving = np.conj(fourier) @ (phase[:, None] * fourier)
    parts = [[matrix.real, matrix.imag] for matrix in (moving, fourier)]
    return np.array(parts, dtype=np.float32)


def halves(values):
    high = values.astype(jnp.bfloat16)
    low = (values - high.astype(jnp.float32)).astype(jnp.bfloat16)
    return high, low


def transform(real, imag, right, left):
    width = real.shape[0]
    high, low = halves(jnp.concatenate([real, imag], axis=1))
    rows = jnp.dot(
        jnp.concatenate([high, low, high], axis=1), right, preferred_element_type=jnp.float32
    )
    high, low = halves(jnp.concatenate([rows[:, :width], rows[:, width:]], axis=0))
    both = jnp.dot(
        left, jnp.concatenate([high, low, high], axis=0), preferred_element_type=jnp.float32
    )
    return both[:width], both[width:]


def times(a, b):
    return a[0] * b[0] - a[1] * b[1], a[0] * b[1] + a[1] * b[0]


def kernel(
    x_ref,
    y_ref,
    mode_ref,
    objects_hbm,
    probes_hbm,
    measured_hbm,
    tables_hbm,
    updated_hbm,
    objects,
    probes,
    measured,
    tables_f32,
    right,
    left,
    total,
    place,
    place_before,
    packed,
    beyond,
    pieces,
    returned,
    load_sem,
    place_sem,
    object_sem,
    piece_sem,
    store_sem,
):
    slices, _, tile, span = objects.shape
    amount, width, _ = measured.shape
    me, devices = lax.axis_index("lat"), lax.axis_size("lat")
    has_before, has_after = me > 0, me < devices - 1
    before, after = jnp.maximum(me - 1, 0), jnp.minimum(me + 1, devices - 1)

    def send(source, target, sems, towards):
        return pltpu.make_async_remote_copy(
            src_ref=source,
            dst_ref=target,
            send_sem=sems[0],
            recv_sem=sems[1],
            device_id={"lat": towards},
            device_id_type=pl.DeviceIdType.MESH,
        )

    def send_place():
        return send(place, place_before, (place_sem.at[0], place_sem.at[1]), after)

    def send_objects(p, s):
        sems = (object_sem.at[0, p, s], object_sem.at[1, p, s])
        return send(packed.at[p, s], beyond.at[p, s], sems, before)

    def send_piece(p, s):
        sems = (piece_sem.at[0, p, s], piece_sem.at[1, p, s])
        return send(pieces.at[p, s], returned.at[p, s], sems, after)

    load_objects = pltpu.make_async_copy(objects_hbm, objects, load_sem.at[0])
    others = [
        pltpu.make_async_copy(source, target, load_sem.at[i + 1])
        for i, (source, target) in enumerate(
            [(tables_hbm, tables_f32), (probes_hbm, probes), (measured_hbm, measured)]
        )
    ]
    load_objects.start()
    for p in range(amount):
        place[p] = jnp.full((1, width), x_ref[p], jnp.int32)
        place[amount + p] = jnp.full((1, width), y_ref[p], jnp.int32)

    barrier = pltpu.get_barrier_semaphore()

    @pl.when(has_before)
    def _():
        pl.semaphore_signal(
            barrier, inc=1, device_id={"lat": before}, device_id_type=pl.DeviceIdType.MESH
        )

    @pl.when(has_after)
    def _():
        pl.semaphore_signal(
            barrier, inc=1, device_id={"lat": after}, device_id_type=pl.DeviceIdType.MESH
        )

    peers = has_before.astype(jnp.int32) + has_after.astype(jnp.int32)
    pl.semaphore_wait(barrier, peers)

    @pl.when(has_after)
    def _():
        send_place().start()

    row = lax.broadcasted_iota(jnp.int32, (width, width), 0)
    column = lax.broadcasted_iota(jnp.int32, (width, width), 1)

    def across(y, k):
        return (column + k * width >= y) & (column + k * width < y + width)

    def gathered(y, s, c):
        value = objects[s, c, :, 0:width]
        for k in range(1, span // width):
            value = jnp.where(across(y, k), objects[s, c, :, k * width : (k + 1) * width], value)
        return value

    load_objects.wait()

    @pl.when(has_before)
    def _():
        send_place().wait_recv()

        def pack(p, carry):
            y = place_before[amount + p]
            for s in range(slices):
                for c in range(2):
                    packed[p, s, c] = gathered(y, s, c)

                @pl.when(p == 0)
                def _():
                    send_objects(p, s).start()

            return carry

        lax.fori_loop(0, amount, pack, 0)

    for copy in others:
        copy.start()

    @pl.when(jnp.logical_not(has_after))
    def _():
        beyond[...] = jnp.zeros_like(beyond)

    for copy in others:
        copy.wait()

    for i in range(2):
        for c, sign in ((0, 1.0), (1, 1.0), (1, -1.0)):
            high, low = halves(sign * tables_f32[i, c])
            for k, part in enumerate((high, high, low)):
                base = 2 * width * k
                near, further = pl.ds(base, width), pl.ds(base + width, width)
                first, second = pl.ds(0, width), pl.ds(width, width)
                if c == 0:
                    right[i, near, first] = part
                    right[i, further, second] = part
                    left[i, first, near] = part
                    left[i, second, further] = part
                elif sign > 0:
                    right[i, near, second] = part
                    left[i, second, near] = part
                else:
                    right[i, further, first] = part
                    left[i, first, further] = part

    def visit(p, carry):
        @pl.when(has_before & (p + 1 < amount))
        def _():
            for s in range(slices):
                send_objects(p, s).wait_send()
                send_objects(p + 1, s).start()

        x, y, mode = x_ref[p], y_ref[p], mode_ref[p]
        inside = row >= x
        shift = lax.rem(y, width)
        entry = [pltpu.roll(pltpu.roll(probes[mode, c], x, 0), shift, 1) for c in range(2)]

        def window(s):
            own = [gathered(y, s, c) for c in range(2)]

            @pl.when(has_after)
            def _():
                send_objects(p, s).wait_recv()

            return [jnp.where(inside, own[c], beyond[p, s, c]) for c in range(2)]

        def emit(s, piece):
            pieces[p, s, 0] = piece[0]
            pieces[p, s, 1] = -piece[1]

            @pl.when(has_after & (p == amount - 1))
            def _():
                send_piece(p, s).start()

        move, far = (right[0], left[0]), (right[1], left[1])
        middle = transform(*times(entry, window(0)), *move)
        slab = window(1)

        @pl.when(has_after & (p > 0))
        def _():
            for s in reversed(range(slices)):
                send_piece(p - 1, s).start()

        psi = transform(*times(middle, slab), *far)
        residual = psi[0] * psi[0] + psi[1] * psi[1] - measured[p]
        back = transform(residual * psi[0], -(residual * psi[1]), *far)
        emit(1, times(middle, back))
        back = transform(*times(slab, back), *move)
        emit(0, times(entry, back))
        return carry

    lax.fori_loop(0, amount, visit, 0)

    def own_update(s, carry):
        for c in range(2):
            for k in range(span // width):
                value = objects[s, c, :, k * width : (k + 1) * width]
                for p in range(amount):
                    mask = across(y_ref[p], k) & (row >= x_ref[p])
                    value = value - descent_rate * jnp.where(mask, pieces[p, s, c], 0.0)
                total[s, c, :, k * width : (k + 1) * width] = value
        return carry

    lax.fori_loop(0, slices, own_update, 0)

    def store(s):
        return pltpu.make_async_copy(total.at[s], updated_hbm.at[s], store_sem.at[s])

    def late_update(step, carry):
        p, s = step // slices, slices - 1 - step % slices

        @pl.when(has_before)
        def _():
            send_piece(p, s).wait_recv()
            x, y = place_before[p], place_before[amount + p]
            inside = row < x
            for c in range(2):
                piece = jnp.where(inside, returned[p, s, c], 0.0)
                for k in range(span // width):
                    kept = jnp.where(across(y, k), piece, 0.0)
                    where = (s, c, slice(None), slice(k * width, (k + 1) * width))
                    total[where] = total[where] - descent_rate * kept

        @pl.when(p == amount - 1)
        def _():
            store(s).start()

        return carry

    lax.fori_loop(0, amount * slices, late_update, 0)

    for s in range(slices):

        @pl.when(has_before)
        def _():
            send_objects(amount - 1, s).wait_send()

        for p in range(amount):

            @pl.when(has_after)
            def _():
                send_piece(p, s).wait_send()

    @pl.when(has_after)
    def _():
        send_place().wait_send()

    for s in range(slices):
        store(s).wait()


def on_device(objects, probes, x_offsets, y_offsets, modes, measured):
    slices = objects.shape[0]
    amount, width, _ = measured.shape
    factors = jnp.asarray(tables(width))
    windows = (amount, slices, 2, width, width)
    small = pl.BlockSpec(memory_space=pltpu.SMEM)
    large = pl.BlockSpec(memory_space=pltpu.HBM)
    return pl.pallas_call(
        kernel,
        out_shape=pltpu.VMEM(objects.shape, jnp.float32),
        in_specs=[small] * 3 + [large] * 4,
        out_specs=pl.BlockSpec(memory_space=pl.ANY),
        scratch_shapes=[
            pltpu.VMEM(objects.shape, jnp.float32),
            pltpu.VMEM(probes.shape, jnp.float32),
            pltpu.VMEM(measured.shape, jnp.float32),
            pltpu.VMEM(factors.shape, jnp.float32),
            pltpu.VMEM((2, 6 * width, 2 * width), jnp.bfloat16),
            pltpu.VMEM((2, 2 * width, 6 * width), jnp.bfloat16),
            pltpu.VMEM(objects.shape, jnp.float32),
            pltpu.VMEM((2 * amount, 1, width), jnp.int32),
            pltpu.VMEM((2 * amount, 1, width), jnp.int32),
            pltpu.VMEM(windows, jnp.float32),
            pltpu.VMEM(windows, jnp.float32),
            pltpu.VMEM(windows, jnp.float32),
            pltpu.VMEM(windows, jnp.float32),
            pltpu.SemaphoreType.DMA((4,)),
            pltpu.SemaphoreType.DMA((2,)),
            pltpu.SemaphoreType.DMA((2, amount, slices)),
            pltpu.SemaphoreType.DMA((2, amount, slices)),
            pltpu.SemaphoreType.DMA((slices,)),
        ],
        compiler_params=pltpu.CompilerParams(
            collective_id=0, has_side_effects=True, vmem_limit_bytes=VMEM_BYTES
        ),
        cost_estimate=pl.CostEstimate(
            flops=amount * 8 * 2 * 6 * 2 * width**3, bytes_accessed=16 << 20, transcendentals=0
        ),
        name="gradient_step",
    )(x_offsets, y_offsets, modes, objects, probes, measured, factors)


def solution(mesh):
    in_specs = (
        P(None, None, ("groups", "lat"), None),
        P("groups", None, None, None),
        P(("groups", "lat")),
        P(("groups", "lat")),
        P(("groups", "lat")),
        P(("groups", "lat"), None, None),
    )
    out_specs = P(None, None, ("groups", "lat"), None)
    return jax.shard_map(
        on_device, mesh=mesh, in_specs=in_specs, out_specs=out_specs, check_vma=False
    )
```

```python
import jax
import jax.numpy as jnp
import numpy as np
from jax import lax
from jax.experimental import pallas as pl
from jax.experimental.pallas import tpu as pltpu
from jax.sharding import PartitionSpec as P

spread_phase = 40.0
descent_rate = 1.0
VMEM_BYTES = 59 * 1024 * 1024


def tables(width):
    counter = np.arange(width)
    fourier = np.exp(-2j * np.pi * (np.outer(counter, counter) % width) / width) / np.sqrt(width)
    folded = ((counter + width // 2) % width - width // 2) / width
    phase = np.exp(-1j * spread_phase * folded**2)
    moving = np.conj(fourier) @ (phase[:, None] * fourier)
    parts = [[matrix.real, matrix.imag] for matrix in (moving, fourier)]
    return np.array(parts, dtype=np.float32)


def halves(values):
    high = values.astype(jnp.bfloat16)
    low = (values - high.astype(jnp.float32)).astype(jnp.bfloat16)
    return high, low


def transform(real, imag, right, left):
    width = real.shape[0]
    high, low = halves(jnp.concatenate([real, imag], axis=1))
    rows = jnp.dot(
        jnp.concatenate([high, low, high], axis=1), right, preferred_element_type=jnp.float32
    )
    high, low = halves(jnp.concatenate([rows[:, :width], rows[:, width:]], axis=0))
    both = jnp.dot(
        left, jnp.concatenate([high, low, high], axis=0), preferred_element_type=jnp.float32
    )
    return both[:width], both[width:]


def times(a, b):
    return a[0] * b[0] - a[1] * b[1], a[0] * b[1] + a[1] * b[0]


def kernel(
    x_ref,
    y_ref,
    mode_ref,
    objects_hbm,
    probes_hbm,
    measured_hbm,
    tables_hbm,
    total,
    objects,
    probes,
    measured,
    tables_f32,
    right,
    left,
    place,
    place_before,
    packed,
    beyond,
    pieces,
    returned,
    object_load_sem,
    load_sem,
    place_sem,
    object_sem,
    piece_sem,
):
    slices, _, tile, span = objects.shape
    amount, width, _ = measured.shape
    me, devices = lax.axis_index("lat"), lax.axis_size("lat")
    has_before, has_after = me > 0, me < devices - 1
    before, after = jnp.maximum(me - 1, 0), jnp.minimum(me + 1, devices - 1)

    def send(source, target, sems, towards):
        return pltpu.make_async_remote_copy(
            src_ref=source,
            dst_ref=target,
            send_sem=sems[0],
            recv_sem=sems[1],
            device_id={"lat": towards},
            device_id_type=pl.DeviceIdType.MESH,
        )

    def send_place():
        return send(place, place_before, (place_sem.at[0], place_sem.at[1]), after)

    def send_objects(p, s):
        sems = (object_sem.at[0, p, s], object_sem.at[1, p, s])
        return send(packed.at[p, s], beyond.at[p, s], sems, before)

    def send_piece(p, s):
        sems = (piece_sem.at[0, p, s], piece_sem.at[1, p, s])
        return send(pieces.at[p, s], returned.at[p, s], sems, after)

    load_objects = [
        pltpu.make_async_copy(objects_hbm.at[s], objects.at[s], object_load_sem.at[s])
        for s in range(slices)
    ]
    others = [
        pltpu.make_async_copy(source, target, load_sem.at[i])
        for i, (source, target) in enumerate(
            [(tables_hbm, tables_f32), (probes_hbm, probes), (measured_hbm, measured)]
        )
    ]
    for copy in load_objects:
        copy.start()
    for p in range(amount):
        place[p] = jnp.full((1, width), x_ref[p], jnp.int32)
        place[amount + p] = jnp.full((1, width), y_ref[p], jnp.int32)

    barrier = pltpu.get_barrier_semaphore()

    @pl.when(has_before)
    def _():
        pl.semaphore_signal(
            barrier, inc=1, device_id={"lat": before}, device_id_type=pl.DeviceIdType.MESH
        )

    @pl.when(has_after)
    def _():
        pl.semaphore_signal(
            barrier, inc=1, device_id={"lat": after}, device_id_type=pl.DeviceIdType.MESH
        )

    peers = has_before.astype(jnp.int32) + has_after.astype(jnp.int32)
    pl.semaphore_wait(barrier, peers)

    @pl.when(has_after)
    def _():
        send_place().start()

    row = lax.broadcasted_iota(jnp.int32, (width, width), 0)
    column = lax.broadcasted_iota(jnp.int32, (width, width), 1)

    def across(y, k):
        return (column + k * width >= y) & (column + k * width < y + width)

    def gathered(y, s, c):
        value = objects[s, c, :, 0:width]
        for k in range(1, span // width):
            value = jnp.where(across(y, k), objects[s, c, :, k * width : (k + 1) * width], value)
        return value

    @pl.when(has_before)
    def _():
        send_place().wait_recv()

    for p in range(amount):
        for s in range(slices):
            if p == 0:
                load_objects[s].wait()

            @pl.when(has_before)
            def _():
                y = place_before[amount + p]
                for c in range(2):
                    packed[p, s, c] = gathered(y, s, c)
                if p == 0:
                    send_objects(p, s).start()

    for copy in others:
        copy.start()

    @pl.when(jnp.logical_not(has_after))
    def _():
        beyond[...] = jnp.zeros_like(beyond)

    for copy in others:
        copy.wait()

    for i in range(2):
        for c, sign in ((0, 1.0), (1, 1.0), (1, -1.0)):
            high, low = halves(sign * tables_f32[i, c])
            for k, part in enumerate((high, high, low)):
                base = 2 * width * k
                near, further = pl.ds(base, width), pl.ds(base + width, width)
                first, second = pl.ds(0, width), pl.ds(width, width)
                if c == 0:
                    right[i, near, first] = part
                    right[i, further, second] = part
                    left[i, first, near] = part
                    left[i, second, further] = part
                elif sign > 0:
                    right[i, near, second] = part
                    left[i, second, near] = part
                else:
                    right[i, further, first] = part
                    left[i, first, further] = part

    def visit(p, carry):
        @pl.when(has_before & (p + 1 < amount))
        def _():
            for s in range(slices):
                send_objects(p, s).wait_send()
                send_objects(p + 1, s).start()

        x, y, mode = x_ref[p], y_ref[p], mode_ref[p]
        inside = row >= x
        shift = lax.rem(y, width)
        entry = [pltpu.roll(pltpu.roll(probes[mode, c], x, 0), shift, 1) for c in range(2)]

        @pl.when(has_after)
        def _():
            for s in range(slices):
                send_objects(p, s).wait_recv()

        @pl.when(has_after & (p > 0))
        def _():
            for s in reversed(range(slices)):
                send_piece(p - 1, s).start()

        def window(s):
            own = [gathered(y, s, c) for c in range(2)]
            return [jnp.where(inside, own[c], beyond[p, s, c]) for c in range(2)]

        def emit(s, piece):
            pieces[p, s, 0] = piece[0]
            pieces[p, s, 1] = -piece[1]

            if s > 0 or amount == 1:

                @pl.when(has_after & (p == amount - 1))
                def _():
                    send_piece(p, s).start()

        move, far = (right[0], left[0]), (right[1], left[1])
        middle = transform(*times(entry, window(0)), *move)
        slab = window(1)
        psi = transform(*times(middle, slab), *far)
        residual = psi[0] * psi[0] + psi[1] * psi[1] - measured[p]
        back = transform(residual * psi[0], -(residual * psi[1]), *far)
        emit(1, times(middle, back))
        back = transform(*times(slab, back), *move)
        emit(0, times(entry, back))
        return carry

    lax.fori_loop(0, amount, visit, 0)

    def own_update(s, carry):
        for c in range(2):
            for k in range(span // width):
                value = objects[s, c, :, k * width : (k + 1) * width]
                for p in range(amount):
                    mask = across(y_ref[p], k) & (row >= x_ref[p])
                    value = value - descent_rate * jnp.where(mask, pieces[p, s, c], 0.0)
                total[s, c, :, k * width : (k + 1) * width] = value
        return carry

    lax.fori_loop(0, slices, own_update, 0)

    if amount > 1:

        @pl.when(has_after)
        def _():
            for s in reversed(range(slices)):
                send_piece(amount - 2, s).wait_send()
            send_piece(amount - 1, 0).start()

    def late_update(step, carry):
        p, s = step // slices, slices - 1 - step % slices

        @pl.when(has_before)
        def _():
            send_piece(p, s).wait_recv()
            x, y = place_before[p], place_before[amount + p]
            inside = row < x
            for c in range(2):
                piece = jnp.where(inside, returned[p, s, c], 0.0)
                for k in range(span // width):
                    kept = jnp.where(across(y, k), piece, 0.0)
                    where = (s, c, slice(None), slice(k * width, (k + 1) * width))
                    total[where] = total[where] - descent_rate * kept

        return carry

    lax.fori_loop(0, amount * slices, late_update, 0)

    for s in range(slices):

        @pl.when(has_before)
        def _():
            send_objects(amount - 1, s).wait_send()

        for p in range(amount):
            if p != amount - 2:

                @pl.when(has_after)
                def _():
                    send_piece(p, s).wait_send()

    @pl.when(has_after)
    def _():
        send_place().wait_send()


def on_device(objects, probes, x_offsets, y_offsets, modes, measured):
    slices = objects.shape[0]
    amount, width, _ = measured.shape
    factors = jnp.asarray(tables(width))
    windows = (amount, slices, 2, width, width)
    small = pl.BlockSpec(memory_space=pltpu.SMEM)
    large = pl.BlockSpec(memory_space=pltpu.HBM)
    return pl.pallas_call(
        kernel,
        out_shape=pltpu.VMEM(objects.shape, jnp.float32),
        in_specs=[small] * 3 + [large] * 4,
        out_specs=pl.BlockSpec(memory_space=pltpu.VMEM),
        scratch_shapes=[
            pltpu.VMEM(objects.shape, jnp.float32),
            pltpu.VMEM(probes.shape, jnp.float32),
            pltpu.VMEM(measured.shape, jnp.float32),
            pltpu.VMEM(factors.shape, jnp.float32),
            pltpu.VMEM((2, 6 * width, 2 * width), jnp.bfloat16),
            pltpu.VMEM((2, 2 * width, 6 * width), jnp.bfloat16),
            pltpu.VMEM((2 * amount, 1, width), jnp.int32),
            pltpu.VMEM((2 * amount, 1, width), jnp.int32),
            pltpu.VMEM(windows, jnp.float32),
            pltpu.VMEM(windows, jnp.float32),
            pltpu.VMEM(windows, jnp.float32),
            pltpu.VMEM(windows, jnp.float32),
            pltpu.SemaphoreType.DMA((slices,)),
            pltpu.SemaphoreType.DMA((3,)),
            pltpu.SemaphoreType.DMA((2,)),
            pltpu.SemaphoreType.DMA((2, amount, slices)),
            pltpu.SemaphoreType.DMA((2, amount, slices)),
        ],
        compiler_params=pltpu.CompilerParams(
            collective_id=0, has_side_effects=True, vmem_limit_bytes=VMEM_BYTES
        ),
        cost_estimate=pl.CostEstimate(
            flops=amount * 8 * 2 * 6 * 2 * width**3, bytes_accessed=16 << 20, transcendentals=0
        ),
        name="gradient_step",
    )(x_offsets, y_offsets, modes, objects, probes, measured, factors)


def solution(mesh):
    in_specs = (
        P(None, None, ("groups", "lat"), None),
        P("groups", None, None, None),
        P(("groups", "lat")),
        P(("groups", "lat")),
        P(("groups", "lat")),
        P(("groups", "lat"), None, None),
    )
    out_specs = P(None, None, ("groups", "lat"), None)
    return jax.shard_map(
        on_device, mesh=mesh, in_specs=in_specs, out_specs=out_specs, check_vma=False
    )
```

```python
import jax
import jax.numpy as jnp
import numpy as np
from jax import lax
from jax.experimental import pallas as pl
from jax.experimental.pallas import tpu as pltpu
from jax.sharding import PartitionSpec as P

spread_phase = 40.0
descent_rate = 1.0
VMEM_BYTES = 59 * 1024 * 1024


def tables(width):
    counter = np.arange(width)
    fourier = np.exp(-2j * np.pi * (np.outer(counter, counter) % width) / width) / np.sqrt(width)
    folded = ((counter + width // 2) % width - width // 2) / width
    phase = np.exp(-1j * spread_phase * folded**2)
    moving = np.conj(fourier) @ (phase[:, None] * fourier)
    parts = [[matrix.real, matrix.imag] for matrix in (moving, fourier)]
    return np.array(parts, dtype=np.float32)


def halves(values):
    high = values.astype(jnp.bfloat16)
    low = (values - high.astype(jnp.float32)).astype(jnp.bfloat16)
    return high, low


def transform(real, imag, right, left):
    width = real.shape[0]
    high, low = halves(jnp.concatenate([real, imag], axis=1))
    rows = jnp.dot(
        jnp.concatenate([high, low, high], axis=1), right, preferred_element_type=jnp.float32
    )
    high, low = halves(jnp.concatenate([rows[:, :width], rows[:, width:]], axis=0))
    both = jnp.dot(
        left, jnp.concatenate([high, low, high], axis=0), preferred_element_type=jnp.float32
    )
    return both[:width], both[width:]


def times(a, b):
    return a[0] * b[0] - a[1] * b[1], a[0] * b[1] + a[1] * b[0]


def kernel(
    x_hbm,
    y_hbm,
    mode_hbm,
    objects_hbm,
    probes_hbm,
    measured_hbm,
    tables_hbm,
    total,
    x_ref,
    y_ref,
    mode_ref,
    objects,
    probes,
    measured,
    tables_f32,
    right,
    left,
    place,
    place_before,
    packed,
    beyond,
    pieces,
    returned,
    scalar_sem,
    object_load_sem,
    load_sem,
    place_sem,
    object_sem,
    piece_sem,
):
    slices, _, tile, span = objects.shape
    amount, width, _ = measured.shape
    me, devices = lax.axis_index("lat"), lax.axis_size("lat")
    has_before, has_after = me > 0, me < devices - 1
    before, after = jnp.maximum(me - 1, 0), jnp.minimum(me + 1, devices - 1)

    def send(source, target, sems, towards):
        return pltpu.make_async_remote_copy(
            src_ref=source,
            dst_ref=target,
            send_sem=sems[0],
            recv_sem=sems[1],
            device_id={"lat": towards},
            device_id_type=pl.DeviceIdType.MESH,
        )

    def send_place():
        return send(place, place_before, (place_sem.at[0], place_sem.at[1]), after)

    def send_objects(p, s):
        sems = (object_sem.at[0, p, s], object_sem.at[1, p, s])
        return send(packed.at[p, s], beyond.at[p, s], sems, before)

    def send_piece(p, s):
        sems = (piece_sem.at[0, p, s], piece_sem.at[1, p, s])
        return send(pieces.at[p, s], returned.at[p, s], sems, after)

    load_objects = [
        pltpu.make_async_copy(objects_hbm.at[s], objects.at[s], object_load_sem.at[s])
        for s in range(slices)
    ]
    others = [
        pltpu.make_async_copy(source, target, load_sem.at[i])
        for i, (source, target) in enumerate(
            [(tables_hbm, tables_f32), (probes_hbm, probes), (measured_hbm, measured)]
        )
    ]
    load_scalars = [
        pltpu.make_async_copy(source, target, scalar_sem.at[i])
        for i, (source, target) in enumerate(
            [(x_hbm, x_ref), (y_hbm, y_ref), (mode_hbm, mode_ref)]
        )
    ]
    for copy in load_scalars:
        copy.start()
    barrier = pltpu.get_barrier_semaphore()

    @pl.when(has_before)
    def _():
        pl.semaphore_signal(
            barrier, inc=1, device_id={"lat": before}, device_id_type=pl.DeviceIdType.MESH
        )

    @pl.when(has_after)
    def _():
        pl.semaphore_signal(
            barrier, inc=1, device_id={"lat": after}, device_id_type=pl.DeviceIdType.MESH
        )

    for copy in load_objects:
        copy.start()
    for copy in load_scalars:
        copy.wait()
    for p in range(amount):
        place[p] = jnp.full((1, width), x_ref[p], jnp.int32)
        place[amount + p] = jnp.full((1, width), y_ref[p], jnp.int32)

    peers = has_before.astype(jnp.int32) + has_after.astype(jnp.int32)
    pl.semaphore_wait(barrier, peers)

    @pl.when(has_after)
    def _():
        send_place().start()

    row = lax.broadcasted_iota(jnp.int32, (width, width), 0)
    column = lax.broadcasted_iota(jnp.int32, (width, width), 1)

    def across(y, k):
        return (column + k * width >= y) & (column + k * width < y + width)

    def gathered(y, s, c):
        value = objects[s, c, :, 0:width]
        for k in range(1, span // width):
            value = jnp.where(across(y, k), objects[s, c, :, k * width : (k + 1) * width], value)
        return value

    @pl.when(has_before)
    def _():
        send_place().wait_recv()

    for p in range(amount):
        for s in range(slices):
            if p == 0:
                load_objects[s].wait()

            @pl.when(has_before)
            def _():
                y = place_before[amount + p]
                for c in range(2):
                    packed[p, s, c] = gathered(y, s, c)
                if p == 0:
                    send_objects(p, s).start()

    for copy in others:
        copy.start()

    @pl.when(jnp.logical_not(has_after))
    def _():
        beyond[...] = jnp.zeros_like(beyond)

    for copy in others:
        copy.wait()

    for i in range(2):
        for c, sign in ((0, 1.0), (1, 1.0), (1, -1.0)):
            high, low = halves(sign * tables_f32[i, c])
            for k, part in enumerate((high, high, low)):
                base = 2 * width * k
                near, further = pl.ds(base, width), pl.ds(base + width, width)
                first, second = pl.ds(0, width), pl.ds(width, width)
                if c == 0:
                    right[i, near, first] = part
                    right[i, further, second] = part
                    left[i, first, near] = part
                    left[i, second, further] = part
                elif sign > 0:
                    right[i, near, second] = part
                    left[i, second, near] = part
                else:
                    right[i, further, first] = part
                    left[i, first, further] = part

    def visit(p, carry):
        @pl.when(has_before & (p + 1 < amount))
        def _():
            for s in range(slices):
                send_objects(p, s).wait_send()
                send_objects(p + 1, s).start()

        x, y, mode = x_ref[p], y_ref[p], mode_ref[p]
        inside = row >= x
        shift = lax.rem(y, width)
        entry = [pltpu.roll(pltpu.roll(probes[mode, c], x, 0), shift, 1) for c in range(2)]

        @pl.when(has_after)
        def _():
            send_objects(p, 0).wait_recv()

        @pl.when(has_after & (p > 0))
        def _():
            for s in reversed(range(slices)):
                send_piece(p - 1, s).start()

        @pl.when(has_after)
        def _():
            for s in range(1, slices):
                send_objects(p, s).wait_recv()

        def window(s):
            own = [gathered(y, s, c) for c in range(2)]
            return [jnp.where(inside, own[c], beyond[p, s, c]) for c in range(2)]

        def emit(s, piece):
            pieces[p, s, 0] = piece[0]
            pieces[p, s, 1] = -piece[1]

            if s > 0 or amount == 1:

                @pl.when(has_after & (p == amount - 1))
                def _():
                    send_piece(p, s).start()

        move, far = (right[0], left[0]), (right[1], left[1])
        middle = transform(*times(entry, window(0)), *move)
        slab = window(1)
        psi = transform(*times(middle, slab), *far)
        residual = psi[0] * psi[0] + psi[1] * psi[1] - measured[p]
        back = transform(residual * psi[0], -(residual * psi[1]), *far)
        emit(1, times(middle, back))
        back = transform(*times(slab, back), *move)
        emit(0, times(entry, back))
        return carry

    lax.fori_loop(0, amount, visit, 0)

    def own_update(s, carry):
        for c in range(2):
            for k in range(span // width):
                value = objects[s, c, :, k * width : (k + 1) * width]
                for p in range(amount):
                    mask = across(y_ref[p], k) & (row >= x_ref[p])
                    value = value - descent_rate * jnp.where(mask, pieces[p, s, c], 0.0)
                total[s, c, :, k * width : (k + 1) * width] = value
        return carry

    lax.fori_loop(0, slices, own_update, 0)

    if amount > 1:

        @pl.when(has_after)
        def _():
            for s in reversed(range(slices)):
                send_piece(amount - 2, s).wait_send()
            send_piece(amount - 1, 0).start()

    def late_update(step, carry):
        p, s = step // slices, slices - 1 - step % slices

        @pl.when(has_before)
        def _():
            send_piece(p, s).wait_recv()
            x, y = place_before[p], place_before[amount + p]
            inside = row < x
            for c in range(2):
                piece = jnp.where(inside, returned[p, s, c], 0.0)
                for k in range(span // width):
                    kept = jnp.where(across(y, k), piece, 0.0)
                    where = (s, c, slice(None), slice(k * width, (k + 1) * width))
                    total[where] = total[where] - descent_rate * kept

        return carry

    lax.fori_loop(0, amount * slices, late_update, 0)

    for s in range(slices):

        @pl.when(has_before)
        def _():
            send_objects(amount - 1, s).wait_send()

        for p in range(amount):
            if p != amount - 2:

                @pl.when(has_after)
                def _():
                    send_piece(p, s).wait_send()

    @pl.when(has_after)
    def _():
        send_place().wait_send()


def on_device(objects, probes, x_offsets, y_offsets, modes, measured):
    slices = objects.shape[0]
    amount, width, _ = measured.shape
    factors = jnp.asarray(tables(width))
    windows = (amount, slices, 2, width, width)
    large = pl.BlockSpec(memory_space=pltpu.HBM)
    return pl.pallas_call(
        kernel,
        out_shape=pltpu.VMEM(objects.shape, jnp.float32),
        in_specs=[large] * 7,
        out_specs=pl.BlockSpec(memory_space=pltpu.VMEM),
        scratch_shapes=[
            pltpu.SMEM(x_offsets.shape, jnp.int32),
            pltpu.SMEM(y_offsets.shape, jnp.int32),
            pltpu.SMEM(modes.shape, jnp.int32),
            pltpu.VMEM(objects.shape, jnp.float32),
            pltpu.VMEM(probes.shape, jnp.float32),
            pltpu.VMEM(measured.shape, jnp.float32),
            pltpu.VMEM(factors.shape, jnp.float32),
            pltpu.VMEM((2, 6 * width, 2 * width), jnp.bfloat16),
            pltpu.VMEM((2, 2 * width, 6 * width), jnp.bfloat16),
            pltpu.VMEM((2 * amount, 1, width), jnp.int32),
            pltpu.VMEM((2 * amount, 1, width), jnp.int32),
            pltpu.VMEM(windows, jnp.float32),
            pltpu.VMEM(windows, jnp.float32),
            pltpu.VMEM(windows, jnp.float32),
            pltpu.VMEM(windows, jnp.float32),
            pltpu.SemaphoreType.DMA((3,)),
            pltpu.SemaphoreType.DMA((slices,)),
            pltpu.SemaphoreType.DMA((3,)),
            pltpu.SemaphoreType.DMA((2,)),
            pltpu.SemaphoreType.DMA((2, amount, slices)),
            pltpu.SemaphoreType.DMA((2, amount, slices)),
        ],
        compiler_params=pltpu.CompilerParams(
            collective_id=0, has_side_effects=True, vmem_limit_bytes=VMEM_BYTES
        ),
        cost_estimate=pl.CostEstimate(
            flops=amount * 8 * 2 * 6 * 2 * width**3, bytes_accessed=16 << 20, transcendentals=0
        ),
        name="gradient_step",
    )(x_offsets, y_offsets, modes, objects, probes, measured, factors)


def solution(mesh):
    in_specs = (
        P(None, None, ("groups", "lat"), None),
        P("groups", None, None, None),
        P(("groups", "lat")),
        P(("groups", "lat")),
        P(("groups", "lat")),
        P(("groups", "lat"), None, None),
    )
    out_specs = P(None, None, ("groups", "lat"), None)
    return jax.shard_map(
        on_device, mesh=mesh, in_specs=in_specs, out_specs=out_specs, check_vma=False
    )
```

```python
import jax
import jax.numpy as jnp
import numpy as np
from jax import lax
from jax.experimental import pallas as pl
from jax.experimental.pallas import tpu as pltpu
from jax.sharding import PartitionSpec as P

spread_phase = 40.0
descent_rate = 1.0
VMEM_BYTES = 59 * 1024 * 1024


def tables(width):
    counter = np.arange(width)
    fourier = np.exp(-2j * np.pi * (np.outer(counter, counter) % width) / width) / np.sqrt(width)
    folded = ((counter + width // 2) % width - width // 2) / width
    phase = np.exp(-1j * spread_phase * folded**2)
    moving = np.conj(fourier) @ (phase[:, None] * fourier)
    parts = [[matrix.real, matrix.imag] for matrix in (moving, fourier)]
    return np.array(parts, dtype=np.float32)


def halves(values):
    high = values.astype(jnp.bfloat16)
    low = (values - high.astype(jnp.float32)).astype(jnp.bfloat16)
    return high, low


def transform(real, imag, right, left):
    width = real.shape[0]
    high, low = halves(jnp.concatenate([real, imag], axis=1))
    rows = jnp.dot(
        jnp.concatenate([high, low, high], axis=1), right, preferred_element_type=jnp.float32
    )
    high, low = halves(jnp.concatenate([rows[:, :width], rows[:, width:]], axis=0))
    both = jnp.dot(
        left, jnp.concatenate([high, low, high], axis=0), preferred_element_type=jnp.float32
    )
    return both[:width], both[width:]


def times(a, b):
    return a[0] * b[0] - a[1] * b[1], a[0] * b[1] + a[1] * b[0]


def kernel(
    x_hbm,
    y_hbm,
    mode_hbm,
    objects_hbm,
    probes_hbm,
    measured_hbm,
    tables_hbm,
    total,
    x_ref,
    y_ref,
    mode_ref,
    objects,
    probes,
    measured,
    tables_f32,
    right,
    left,
    place,
    place_before,
    packed,
    beyond,
    pieces,
    returned,
    scalar_sem,
    object_load_sem,
    load_sem,
    place_sem,
    object_sem,
    piece_sem,
):
    slices, _, tile, span = objects.shape
    amount, width, _ = measured.shape
    me, devices = lax.axis_index("lat"), lax.axis_size("lat")
    has_before, has_after = me > 0, me < devices - 1
    before, after = jnp.maximum(me - 1, 0), jnp.minimum(me + 1, devices - 1)

    def send(source, target, sems, towards):
        return pltpu.make_async_remote_copy(
            src_ref=source,
            dst_ref=target,
            send_sem=sems[0],
            recv_sem=sems[1],
            device_id={"lat": towards},
            device_id_type=pl.DeviceIdType.MESH,
        )

    def send_place():
        return send(place, place_before, (place_sem.at[0], place_sem.at[1]), after)

    def send_objects(p, s):
        sems = (object_sem.at[0, p, s], object_sem.at[1, p, s])
        return send(packed.at[p, s], beyond.at[p, s], sems, before)

    def send_piece(p, s):
        sems = (piece_sem.at[0, p, s], piece_sem.at[1, p, s])
        return send(pieces.at[p, s], returned.at[p, s], sems, after)

    load_objects = [
        pltpu.make_async_copy(objects_hbm.at[s], objects.at[s], object_load_sem.at[s])
        for s in range(slices)
    ]
    others = [
        pltpu.make_async_copy(source, target, load_sem.at[i])
        for i, (source, target) in enumerate(
            [(tables_hbm, tables_f32), (probes_hbm, probes), (measured_hbm, measured)]
        )
    ]
    load_scalars = [
        pltpu.make_async_copy(source, target, scalar_sem.at[i])
        for i, (source, target) in enumerate(
            [(x_hbm, x_ref), (y_hbm, y_ref), (mode_hbm, mode_ref)]
        )
    ]
    for copy in load_scalars:
        copy.start()
    barrier = pltpu.get_barrier_semaphore()

    @pl.when(has_before)
    def _():
        pl.semaphore_signal(
            barrier, inc=1, device_id={"lat": before}, device_id_type=pl.DeviceIdType.MESH
        )

    @pl.when(has_after)
    def _():
        pl.semaphore_signal(
            barrier, inc=1, device_id={"lat": after}, device_id_type=pl.DeviceIdType.MESH
        )

    for copy in load_objects:
        copy.start()
    for copy in load_scalars:
        copy.wait()
    for p in range(amount):
        place[p] = jnp.full((1, width), x_ref[p], jnp.int32)
        place[amount + p] = jnp.full((1, width), y_ref[p], jnp.int32)

    peers = has_before.astype(jnp.int32) + has_after.astype(jnp.int32)
    pl.semaphore_wait(barrier, peers)

    @pl.when(has_after)
    def _():
        send_place().start()

    row = lax.broadcasted_iota(jnp.int32, (width, width), 0)
    column = lax.broadcasted_iota(jnp.int32, (width, width), 1)

    def across(y, k):
        return (column + k * width >= y) & (column + k * width < y + width)

    def gathered(y, s, c):
        value = objects[s, c, :, 0:width]
        for k in range(1, span // width):
            value = jnp.where(across(y, k), objects[s, c, :, k * width : (k + 1) * width], value)
        return value

    @pl.when(has_before)
    def _():
        send_place().wait_recv()

    for p in range(amount):
        for s in range(slices):
            if p == 0:
                load_objects[s].wait()

            @pl.when(has_before)
            def _():
                y = place_before[amount + p]
                for c in range(2):
                    packed[p, s, c] = gathered(y, s, c)
                send_objects(p, s).start()

    for copy in others:
        copy.start()

    @pl.when(jnp.logical_not(has_after))
    def _():
        beyond[...] = jnp.zeros_like(beyond)

    for copy in others:
        copy.wait()

    for i in range(2):
        for c, sign in ((0, 1.0), (1, 1.0), (1, -1.0)):
            high, low = halves(sign * tables_f32[i, c])
            for k, part in enumerate((high, high, low)):
                base = 2 * width * k
                near, further = pl.ds(base, width), pl.ds(base + width, width)
                first, second = pl.ds(0, width), pl.ds(width, width)
                if c == 0:
                    right[i, near, first] = part
                    right[i, further, second] = part
                    left[i, first, near] = part
                    left[i, second, further] = part
                elif sign > 0:
                    right[i, near, second] = part
                    left[i, second, near] = part
                else:
                    right[i, further, first] = part
                    left[i, first, further] = part

    def visit(p, carry):
        x, y, mode = x_ref[p], y_ref[p], mode_ref[p]
        inside = row >= x
        shift = lax.rem(y, width)
        entry = [pltpu.roll(pltpu.roll(probes[mode, c], x, 0), shift, 1) for c in range(2)]

        @pl.when(has_after)
        def _():
            for s in range(slices):
                send_objects(p, s).wait_recv()

        @pl.when(has_after & (p > 0))
        def _():
            for s in reversed(range(slices)):
                send_piece(p - 1, s).start()

        def window(s):
            own = [gathered(y, s, c) for c in range(2)]
            return [jnp.where(inside, own[c], beyond[p, s, c]) for c in range(2)]

        def emit(s, piece):
            pieces[p, s, 0] = piece[0]
            pieces[p, s, 1] = -piece[1]

            @pl.when(has_after & (p == amount - 1))
            def _():
                send_piece(p, s).start()

        move, far = (right[0], left[0]), (right[1], left[1])
        middle = transform(*times(entry, window(0)), *move)
        slab = window(1)
        psi = transform(*times(middle, slab), *far)
        residual = psi[0] * psi[0] + psi[1] * psi[1] - measured[p]
        back = transform(residual * psi[0], -(residual * psi[1]), *far)
        emit(1, times(middle, back))
        back = transform(*times(slab, back), *move)
        emit(0, times(entry, back))
        return carry

    lax.fori_loop(0, amount, visit, 0)

    def own_update(s, carry):
        for c in range(2):
            for k in range(span // width):
                value = objects[s, c, :, k * width : (k + 1) * width]
                for p in range(amount):
                    mask = across(y_ref[p], k) & (row >= x_ref[p])
                    value = value - descent_rate * jnp.where(mask, pieces[p, s, c], 0.0)
                total[s, c, :, k * width : (k + 1) * width] = value
        return carry

    lax.fori_loop(0, slices, own_update, 0)

    def late_update(step, carry):
        p, s = step // slices, slices - 1 - step % slices

        @pl.when(has_before)
        def _():
            send_piece(p, s).wait_recv()
            x, y = place_before[p], place_before[amount + p]
            inside = row < x
            for c in range(2):
                piece = jnp.where(inside, returned[p, s, c], 0.0)
                for k in range(span // width):
                    kept = jnp.where(across(y, k), piece, 0.0)
                    where = (s, c, slice(None), slice(k * width, (k + 1) * width))
                    total[where] = total[where] - descent_rate * kept

        return carry

    lax.fori_loop(0, amount * slices, late_update, 0)

    for p in range(amount):
        for s in range(slices):

            @pl.when(has_before)
            def _():
                send_objects(p, s).wait_send()

            @pl.when(has_after)
            def _():
                send_piece(p, s).wait_send()

    @pl.when(has_after)
    def _():
        send_place().wait_send()


def on_device(objects, probes, x_offsets, y_offsets, modes, measured):
    slices = objects.shape[0]
    amount, width, _ = measured.shape
    factors = jnp.asarray(tables(width))
    windows = (amount, slices, 2, width, width)
    large = pl.BlockSpec(memory_space=pltpu.HBM)
    return pl.pallas_call(
        kernel,
        out_shape=pltpu.VMEM(objects.shape, jnp.float32),
        in_specs=[large] * 7,
        out_specs=pl.BlockSpec(memory_space=pltpu.VMEM),
        scratch_shapes=[
            pltpu.SMEM(x_offsets.shape, jnp.int32),
            pltpu.SMEM(y_offsets.shape, jnp.int32),
            pltpu.SMEM(modes.shape, jnp.int32),
            pltpu.VMEM(objects.shape, jnp.float32),
            pltpu.VMEM(probes.shape, jnp.float32),
            pltpu.VMEM(measured.shape, jnp.float32),
            pltpu.VMEM(factors.shape, jnp.float32),
            pltpu.VMEM((2, 6 * width, 2 * width), jnp.bfloat16),
            pltpu.VMEM((2, 2 * width, 6 * width), jnp.bfloat16),
            pltpu.VMEM((2 * amount, 1, width), jnp.int32),
            pltpu.VMEM((2 * amount, 1, width), jnp.int32),
            pltpu.VMEM(windows, jnp.float32),
            pltpu.VMEM(windows, jnp.float32),
            pltpu.VMEM(windows, jnp.float32),
            pltpu.VMEM(windows, jnp.float32),
            pltpu.SemaphoreType.DMA((3,)),
            pltpu.SemaphoreType.DMA((slices,)),
            pltpu.SemaphoreType.DMA((3,)),
            pltpu.SemaphoreType.DMA((2,)),
            pltpu.SemaphoreType.DMA((2, amount, slices)),
            pltpu.SemaphoreType.DMA((2, amount, slices)),
        ],
        compiler_params=pltpu.CompilerParams(
            collective_id=0, has_side_effects=True, vmem_limit_bytes=VMEM_BYTES
        ),
        cost_estimate=pl.CostEstimate(
            flops=amount * 8 * 2 * 6 * 2 * width**3, bytes_accessed=16 << 20, transcendentals=0
        ),
        name="gradient_step",
    )(x_offsets, y_offsets, modes, objects, probes, measured, factors)


def solution(mesh):
    in_specs = (
        P(None, None, ("groups", "lat"), None),
        P("groups", None, None, None),
        P(("groups", "lat")),
        P(("groups", "lat")),
        P(("groups", "lat")),
        P(("groups", "lat"), None, None),
    )
    out_specs = P(None, None, ("groups", "lat"), None)
    return jax.shard_map(
        on_device, mesh=mesh, in_specs=in_specs, out_specs=out_specs, check_vma=False
    )
```

```python
import jax
import jax.numpy as jnp
import numpy as np
from jax import lax
from jax.experimental import pallas as pl
from jax.experimental.pallas import tpu as pltpu
from jax.sharding import PartitionSpec as P

spread_phase = 40.0
descent_rate = 1.0
VMEM_BYTES = 59 * 1024 * 1024


def tables(width):
    counter = np.arange(width)
    fourier = np.exp(-2j * np.pi * (np.outer(counter, counter) % width) / width) / np.sqrt(width)
    folded = ((counter + width // 2) % width - width // 2) / width
    phase = np.exp(-1j * spread_phase * folded**2)
    moving = np.conj(fourier) @ (phase[:, None] * fourier)
    parts = [[matrix.real, matrix.imag] for matrix in (moving, fourier)]
    return np.array(parts, dtype=np.float32)


def halves(values):
    high = values.astype(jnp.bfloat16)
    low = (values - high.astype(jnp.float32)).astype(jnp.bfloat16)
    return high, low


def transform(real, imag, right, left):
    width = real.shape[0]
    high, low = halves(jnp.concatenate([real, imag], axis=1))
    rows = jnp.dot(
        jnp.concatenate([high, low, high], axis=1), right, preferred_element_type=jnp.float32
    )
    high, low = halves(jnp.concatenate([rows[:, :width], rows[:, width:]], axis=0))
    both = jnp.dot(
        left, jnp.concatenate([high, low, high], axis=0), preferred_element_type=jnp.float32
    )
    return both[:width], both[width:]


def times(a, b):
    return a[0] * b[0] - a[1] * b[1], a[0] * b[1] + a[1] * b[0]


def kernel(
    x_hbm,
    y_hbm,
    mode_hbm,
    objects_hbm,
    probes_hbm,
    measured_hbm,
    tables_hbm,
    total,
    x_ref,
    y_ref,
    mode_ref,
    objects,
    probes,
    measured,
    tables_f32,
    right,
    left,
    place,
    place_before,
    packed,
    beyond,
    pieces,
    returned,
    scalar_sem,
    object_load_sem,
    load_sem,
    place_sem,
    object_sem,
    piece_sem,
):
    slices, _, tile, span = objects.shape
    amount, width, _ = measured.shape
    me, devices = lax.axis_index("lat"), lax.axis_size("lat")
    has_before, has_after = me > 0, me < devices - 1
    before, after = jnp.maximum(me - 1, 0), jnp.minimum(me + 1, devices - 1)

    def send(source, target, sems, towards):
        return pltpu.make_async_remote_copy(
            src_ref=source,
            dst_ref=target,
            send_sem=sems[0],
            recv_sem=sems[1],
            device_id={"lat": towards},
            device_id_type=pl.DeviceIdType.MESH,
        )

    def send_place():
        return send(place, place_before, (place_sem.at[0], place_sem.at[1]), after)

    def send_objects(p, s, c):
        sems = (object_sem.at[0, p, s, c], object_sem.at[1, p, s, c])
        return send(packed.at[p, s, c], beyond.at[p, s, c], sems, before)

    def send_piece(p, s, c):
        sems = (piece_sem.at[0, p, s, c], piece_sem.at[1, p, s, c])
        return send(pieces.at[p, s, c], returned.at[p, s, c], sems, after)

    load_objects = [
        pltpu.make_async_copy(objects_hbm.at[s], objects.at[s], object_load_sem.at[s])
        for s in range(slices)
    ]
    others = [
        pltpu.make_async_copy(source, target, load_sem.at[i])
        for i, (source, target) in enumerate(
            [(tables_hbm, tables_f32), (probes_hbm, probes), (measured_hbm, measured)]
        )
    ]
    load_scalars = [
        pltpu.make_async_copy(source, target, scalar_sem.at[i])
        for i, (source, target) in enumerate(
            [(x_hbm, x_ref), (y_hbm, y_ref), (mode_hbm, mode_ref)]
        )
    ]
    for copy in load_scalars:
        copy.start()
    barrier = pltpu.get_barrier_semaphore()

    @pl.when(has_before)
    def _():
        pl.semaphore_signal(
            barrier, inc=1, device_id={"lat": before}, device_id_type=pl.DeviceIdType.MESH
        )

    @pl.when(has_after)
    def _():
        pl.semaphore_signal(
            barrier, inc=1, device_id={"lat": after}, device_id_type=pl.DeviceIdType.MESH
        )

    for copy in load_objects:
        copy.start()
    for copy in load_scalars:
        copy.wait()
    for p in range(amount):
        place[p] = jnp.full((1, width), x_ref[p], jnp.int32)
        place[amount + p] = jnp.full((1, width), y_ref[p], jnp.int32)

    peers = has_before.astype(jnp.int32) + has_after.astype(jnp.int32)
    pl.semaphore_wait(barrier, peers)

    @pl.when(has_after)
    def _():
        send_place().start()

    row = lax.broadcasted_iota(jnp.int32, (width, width), 0)
    column = lax.broadcasted_iota(jnp.int32, (width, width), 1)

    def across(y, k):
        return (column + k * width >= y) & (column + k * width < y + width)

    def gathered(y, s, c):
        value = objects[s, c, :, 0:width]
        for k in range(1, span // width):
            value = jnp.where(across(y, k), objects[s, c, :, k * width : (k + 1) * width], value)
        return value

    @pl.when(has_before)
    def _():
        send_place().wait_recv()

    for p in range(amount):
        for s in range(slices):
            if p == 0:
                load_objects[s].wait()

            @pl.when(has_before)
            def _():
                y = place_before[amount + p]
                for c in range(2):
                    packed[p, s, c] = gathered(y, s, c)
                    send_objects(p, s, c).start()

    for copy in others:
        copy.start()

    @pl.when(jnp.logical_not(has_after))
    def _():
        beyond[...] = jnp.zeros_like(beyond)

    for copy in others:
        copy.wait()

    for i in range(2):
        for c, sign in ((0, 1.0), (1, 1.0), (1, -1.0)):
            high, low = halves(sign * tables_f32[i, c])
            for k, part in enumerate((high, high, low)):
                base = 2 * width * k
                near, further = pl.ds(base, width), pl.ds(base + width, width)
                first, second = pl.ds(0, width), pl.ds(width, width)
                if c == 0:
                    right[i, near, first] = part
                    right[i, further, second] = part
                    left[i, first, near] = part
                    left[i, second, further] = part
                elif sign > 0:
                    right[i, near, second] = part
                    left[i, second, near] = part
                else:
                    right[i, further, first] = part
                    left[i, first, further] = part

    def visit(p, carry):
        x, y, mode = x_ref[p], y_ref[p], mode_ref[p]
        inside = row >= x
        shift = lax.rem(y, width)
        entry = [pltpu.roll(pltpu.roll(probes[mode, c], x, 0), shift, 1) for c in range(2)]

        @pl.when(has_after)
        def _():
            for s in range(slices):
                for c in range(2):
                    send_objects(p, s, c).wait_recv()

        @pl.when(has_after & (p > 0))
        def _():
            for s in reversed(range(slices)):
                for c in range(2):
                    send_piece(p - 1, s, c).start()

        def window(s):
            own = [gathered(y, s, c) for c in range(2)]
            return [jnp.where(inside, own[c], beyond[p, s, c]) for c in range(2)]

        def emit(s, piece):
            pieces[p, s, 0] = piece[0]
            pieces[p, s, 1] = -piece[1]

            @pl.when(has_after & (p == amount - 1))
            def _():
                for c in range(2):
                    send_piece(p, s, c).start()

        move, far = (right[0], left[0]), (right[1], left[1])
        middle = transform(*times(entry, window(0)), *move)
        slab = window(1)
        psi = transform(*times(middle, slab), *far)
        residual = psi[0] * psi[0] + psi[1] * psi[1] - measured[p]
        back = transform(residual * psi[0], -(residual * psi[1]), *far)
        emit(1, times(middle, back))
        back = transform(*times(slab, back), *move)
        emit(0, times(entry, back))
        return carry

    lax.fori_loop(0, amount, visit, 0)

    def own_update(s, carry):
        for c in range(2):
            for k in range(span // width):
                value = objects[s, c, :, k * width : (k + 1) * width]
                for p in range(amount):
                    mask = across(y_ref[p], k) & (row >= x_ref[p])
                    value = value - descent_rate * jnp.where(mask, pieces[p, s, c], 0.0)
                total[s, c, :, k * width : (k + 1) * width] = value
        return carry

    lax.fori_loop(0, slices, own_update, 0)

    def late_update(step, carry):
        p, s = step // slices, slices - 1 - step % slices

        @pl.when(has_before)
        def _():
            x, y = place_before[p], place_before[amount + p]
            inside = row < x
            for c in range(2):
                send_piece(p, s, c).wait_recv()
                piece = jnp.where(inside, returned[p, s, c], 0.0)
                for k in range(span // width):
                    kept = jnp.where(across(y, k), piece, 0.0)
                    where = (s, c, slice(None), slice(k * width, (k + 1) * width))
                    total[where] = total[where] - descent_rate * kept

        return carry

    lax.fori_loop(0, amount * slices, late_update, 0)

    for p in range(amount):
        for s in range(slices):

            @pl.when(has_before)
            def _():
                for c in range(2):
                    send_objects(p, s, c).wait_send()

            @pl.when(has_after)
            def _():
                for c in range(2):
                    send_piece(p, s, c).wait_send()

    @pl.when(has_after)
    def _():
        send_place().wait_send()


def on_device(objects, probes, x_offsets, y_offsets, modes, measured):
    slices = objects.shape[0]
    amount, width, _ = measured.shape
    factors = jnp.asarray(tables(width))
    windows = (amount, slices, 2, width, width)
    large = pl.BlockSpec(memory_space=pltpu.HBM)
    return pl.pallas_call(
        kernel,
        out_shape=pltpu.VMEM(objects.shape, jnp.float32),
        in_specs=[large] * 7,
        out_specs=pl.BlockSpec(memory_space=pltpu.VMEM),
        scratch_shapes=[
            pltpu.SMEM(x_offsets.shape, jnp.int32),
            pltpu.SMEM(y_offsets.shape, jnp.int32),
            pltpu.SMEM(modes.shape, jnp.int32),
            pltpu.VMEM(objects.shape, jnp.float32),
            pltpu.VMEM(probes.shape, jnp.float32),
            pltpu.VMEM(measured.shape, jnp.float32),
            pltpu.VMEM(factors.shape, jnp.float32),
            pltpu.VMEM((2, 6 * width, 2 * width), jnp.bfloat16),
            pltpu.VMEM((2, 2 * width, 6 * width), jnp.bfloat16),
            pltpu.VMEM((2 * amount, 1, width), jnp.int32),
            pltpu.VMEM((2 * amount, 1, width), jnp.int32),
            pltpu.VMEM(windows, jnp.float32),
            pltpu.VMEM(windows, jnp.float32),
            pltpu.VMEM(windows, jnp.float32),
            pltpu.VMEM(windows, jnp.float32),
            pltpu.SemaphoreType.DMA((3,)),
            pltpu.SemaphoreType.DMA((slices,)),
            pltpu.SemaphoreType.DMA((3,)),
            pltpu.SemaphoreType.DMA((2,)),
            pltpu.SemaphoreType.DMA((2, amount, slices, 2)),
            pltpu.SemaphoreType.DMA((2, amount, slices, 2)),
        ],
        compiler_params=pltpu.CompilerParams(
            collective_id=0, has_side_effects=True, vmem_limit_bytes=VMEM_BYTES
        ),
        cost_estimate=pl.CostEstimate(
            flops=amount * 8 * 2 * 6 * 2 * width**3, bytes_accessed=16 << 20, transcendentals=0
        ),
        name="gradient_step",
    )(x_offsets, y_offsets, modes, objects, probes, measured, factors)


def solution(mesh):
    in_specs = (
        P(None, None, ("groups", "lat"), None),
        P("groups", None, None, None),
        P(("groups", "lat")),
        P(("groups", "lat")),
        P(("groups", "lat")),
        P(("groups", "lat"), None, None),
    )
    out_specs = P(None, None, ("groups", "lat"), None)
    return jax.shard_map(
        on_device, mesh=mesh, in_specs=in_specs, out_specs=out_specs, check_vma=False
    )
```
